256 devices in a mesh: freq: 4 (over z_lo), shard: 64 (over x, z_hi, y, core).
Axes of the slice: x: 4, y: 4, z: 8 (z_hi: 2, z_lo: 4; z = z_hi * 4 + z_lo), core: 2. Of those that a mesh axis runs over, the one named last changes fastest.
Arguments:
- vis: float32 [4, 2, 2048, 1024], P('freq', None, 'shard'), may hold values from -6 to 6
- counts: int32 [1024], replicated, may hold values from 1 to 16
- band_start: int32 [1], replicated, may hold values from 0 to 1023
- beam: bfloat16 [4, 64, 2, 1024, 1024], P('freq', 'shard'), may hold values from -0.125 to 0.125
- legendre: bfloat16 [64, 1024, 1024], P('shard'), may hold values from -0.1875 to 0.1875
- cycle_index: int32 [1024], replicated, may hold values from 0 to 1023, each once
Outputs:
- sky_map: float32 [1024, 4096], P('shard')
The draws below stay inside these ranges and needn't reach their ends.
Inputs may be any that keep to these rules, and one draw needn't show every extreme that they name: `cycle_index`: each latitude index appears once.
All inputs are finite; a program needn't handle non-finite values.
Results may differ from the reference program's by a relative error of at most 0.0041.
Values may be sent and summed in bfloat16 or wider, within the bound.
A program may use at most 64 MiB of HBM per device.

```python
import math
import jax
import jax.numpy as jnp
from jax import lax

NB = 1024
NT = 2048
L = 1024
NLAT = 1024
NPHI = 4096
M = 64
N_FREQ = 4


def set_ends(entries, key, low, high):
    longest = entries.shape.index(max(entries.shape))
    spots = []
    for shift in (0, 1):
        where = [jax.random.randint(jax.random.fold_in(key, axis), (), 0, length) for axis, length in enumerate(entries.shape)]
        where[longest] = (where[longest] + shift) % entries.shape[longest]
        spots.append(tuple(where))
    return entries.at[spots[0]].set(low).at[spots[1]].set(high)


def shard_levels(stream_key, dims, cuts, least, largest):
    gain = 1.0
    for position, shards_of in cuts:
        draws = jax.random.uniform(jax.random.fold_in(jax.random.fold_in(stream_key, 6), position), (shards_of,), jnp.float32, least / len(cuts), largest / len(cuts))
        gain = gain * jnp.repeat(jnp.exp(draws), dims[position] // shards_of).reshape((-1,) + (1,) * (len(dims) - 1 - position))
    return gain


def normal_values(rng, shape, scale, limit, split=(), kind=jnp.bfloat16):
    drawn = jax.random.normal(rng, shape, jnp.float32) * scale
    if len(split) > 0:
        drawn = shard_levels(rng, shape, split, -0.22, 0.18) * drawn
    return jnp.clip(drawn, min=-limit, max=limit).astype(kind)


def setup_inputs(seed: int = 0) -> dict:
    arg_keys = jax.random.split(jax.random.key(seed), 7)
    return {
        "vis": normal_values(arg_keys[0], (N_FREQ, 2, NT, NB), 1.0, 6.0, ((0, 4), (2, 64)), jnp.float32),
        "counts": set_ends(jax.random.randint(arg_keys[1], (NB,), 1, 17), jax.random.fold_in(arg_keys[1], 1), 1, 16).astype(jnp.int32),
        "band_start": jax.random.randint(arg_keys[2], (1,), 0, L).astype(jnp.int32),
        "beam": normal_values(arg_keys[3], (N_FREQ, M, 2, L, NB), (2 * NB) ** -0.5, 0.125, ((0, 4), (1, 64))),
        "legendre": normal_values(arg_keys[4], (M, L, NLAT), L ** -0.5, 0.1875, ((0, 64),)),
        "cycle_index": jax.random.permutation(arg_keys[5], NLAT).astype(jnp.int32),
    }


def angle_table(first, count, length):
    mvals = first + jnp.arange(count, dtype=jnp.int32)
    steps = jnp.arange(length, dtype=jnp.int32)
    whole = mvals[:, None] * steps[None, :] % length
    return whole.astype(jnp.float32) * (2.0 * math.pi / length)

def reference(vis, counts, band_start, beam, legendre, cycle_index):
    upper_limit = lax.Precision.HIGHEST
    first = band_start[0]
    modes_total = beam.shape[1]
    time_angle = angle_table(first, modes_total, NT)
    time_cosine = jnp.cos(time_angle)
    time_sine = jnp.sin(time_angle)
    visibility_real = vis[:, 0]
    visibility_imaginary = vis[:, 1]
    real_component = jnp.einsum('og,kgl->kol', time_cosine, visibility_real, precision=upper_limit) + jnp.einsum('og,kgl->kol', time_sine, visibility_imaginary, precision=upper_limit)
    imaginary_component = jnp.einsum('og,kgl->kol', time_cosine, visibility_imaginary, precision=upper_limit) - jnp.einsum('og,kgl->kol', time_sine, visibility_real, precision=upper_limit)
    weight = counts.astype(jnp.float32) * (0.125 / math.sqrt(NT))
    modes = (jnp.stack([real_component, imaginary_component], axis=2) * weight).astype(jnp.bfloat16)

    def project(beam_slice, mode_slice):
        prod = jnp.einsum('kla,ja->kjl', beam_slice.astype(jnp.float32), mode_slice.astype(jnp.float32))
        real_alm = prod[0, 0] + prod[1, 1]
        imag_alm = prod[0, 1] - prod[1, 0]
        return jnp.stack([real_alm, imag_alm], axis=0)
    alm_list = []
    for freq_index in range(vis.shape[0]):
        beam_f = beam[freq_index]
        modes_f = modes[freq_index]
        per_mode = lax.map(lambda k: project(beam_f[k], modes_f[k]), jnp.arange(modes_total, dtype=jnp.int32))
        alm_list.append(per_mode)
    alm = jnp.stack(alm_list, axis=0).astype(jnp.bfloat16)
    chosen = jnp.take(legendre, cycle_index, axis=2).astype(jnp.float32)
    cycle_modes = jnp.einsum('fmkl,mlr->fmkr', alm.astype(jnp.float32), chosen)
    pixel_angle = angle_table(first, modes_total, NPHI)
    pcos = jnp.cos(pixel_angle)
    psin = jnp.sin(pixel_angle)
    scale = 1.0 / math.sqrt(2.0 * modes_total)
    maps = (jnp.einsum('fmr,mp->frp', cycle_modes[:, :, 0], pcos, precision=upper_limit) - jnp.einsum('fmr,mp->frp', cycle_modes[:, :, 1], psin, precision=upper_limit)) * scale
    return lax.optimization_barrier(jnp.sum(maps, axis=0))
```

```python
import functools
import math

import jax
import jax.numpy as jnp
from jax import lax
from jax.experimental import pallas as pl
from jax.experimental.pallas import tpu as pltpu
from jax.sharding import PartitionSpec as P

NT = 2048
NPHI = 4096
F32 = jnp.float32
BF16 = jnp.bfloat16
I32 = jnp.int32


def iota(shape, axis):
    return lax.broadcasted_iota(I32, shape, axis)


def cosine(turns, length):
    half = length // 2
    folded = ((turns + half) & (length - 1)) - half
    x = (length // 4 - jnp.abs(folded)).astype(F32) * (2.0 * math.pi / length)
    square = x * x
    total = jnp.full_like(x, 1.0 / math.factorial(13))
    for power, sign in ((11, -1), (9, 1), (7, -1), (5, 1), (3, -1), (1, 1)):
        total = total * square + sign / math.factorial(power)
    return total * x


def split(value):
    high = value.astype(BF16)
    return high, (value - high.astype(F32)).astype(BF16)


def mode_of(x, zh, y, c):
    return ((x * 2 + zh) * 4 + y) * 2 + c


def body(
    vis_hbm,
    counts_hbm,
    band_ref,
    beam_hbm,
    leg_hbm,
    index_hbm,
    out_ref,
    vis,
    counts,
    beam,
    leg,
    index,
    onehot,
    chosen,
    a_send,
    a_recv,
    b_send,
    b_recv,
    c_send,
    c_recv,
    d_send,
    d_recv,
    turned,
    load_sem,
    a_ssem,
    a_rsem,
    b_ssem,
    b_rsem,
    c_ssem,
    c_rsem,
    d_ssem,
    d_rsem,
):
    f = lax.axis_index("freq")
    s = lax.axis_index("shard")
    x, zh, y, c = s // 16, (s // 8) % 2, (s // 2) % 4, s % 2

    def shard_of(px, pz, py, pc):
        return ((px * 2 + pz) * 4 + py) * 2 + pc

    def plane(d):
        return f, shard_of((x + d // 4) % 4, zh, (y + d % 4) % 4, c)

    def column(df, e):
        return (f + df) % 4, shard_of(x, (zh + e // 2) % 2, y, (c + e % 2) % 2)

    barrier = pltpu.get_barrier_semaphore()
    partners = [plane(d) for d in range(1, 16)]
    partners += [column(q // 4, q % 4) for q in range(1, 16)]
    for partner in partners:
        pl.semaphore_signal(
            barrier, inc=1, device_id=partner, device_id_type=pl.DeviceIdType.MESH
        )

    def load(src, dst, i):
        copy = pltpu.make_async_copy(src, dst, load_sem.at[i])
        copy.start()
        return copy

    loads = [
        load(vis_hbm.at[0], vis, 0),
        load(index_hbm, index, 1),
        load(counts_hbm, counts, 2),
        load(leg_hbm.at[0], leg, 3),
        load(beam_hbm.at[0, 0], beam, 4),
    ]

    first = band_ref[0]

    row, col = iota((128, 256), 0), iota((128, 256), 1)
    d, e, ri = row >> 3, (row >> 1) & 3, row & 1
    k = mode_of((x + (d >> 2)) & 3, (zh + (e >> 1)) & 1, (y + (d & 3)) & 3, (c + e) & 1)
    ri_in = (col >> 5) & 1
    time = s * 32 + (col & 31)
    turns = (first + k) * time + (ri - ri_in) * (NT // 4)
    table_hi, table_lo = split(cosine(turns, NT))
    table = jnp.where(((col >> 6) & 1) == 1, table_lo.astype(F32), table_hi.astype(F32)).astype(BF16)
    loads[0].wait()
    vis_hi, vis_lo = split(vis[...].reshape(64, 1024))
    stream = jnp.concatenate([vis_hi, vis_hi, vis_lo, vis_lo], axis=0)
    a_send[...] = jnp.dot(table, stream, preferred_element_type=F32).reshape(16, 8, 1024)

    pl.semaphore_wait(barrier, 30)

    def send(src, dst, ssem, rsem, target):
        copy = pltpu.make_async_remote_copy(
            src_ref=src,
            dst_ref=dst,
            send_sem=ssem,
            recv_sem=rsem,
            device_id=target,
            device_id_type=pl.DeviceIdType.MESH,
        )
        copy.start()
        return copy

    a_copies = [
        send(a_send.at[d], a_recv.at[d], a_ssem.at[d], a_rsem.at[d], plane(d))
        for d in range(1, 16)
    ]

    loads[1].wait()
    stored = index[...]
    lane = iota((8, 128), 1)
    group = lane >> 4
    pieces = []
    for block in range(4):
        for half in range(2):
            joined = jnp.zeros((8, 128), I32)
            for part in range(8):
                px, py = half * 2 + part // 4, part % 4
                source = py * 2 + block % 2
                line = jnp.broadcast_to(stored[px * 2 + block // 2 : px * 2 + block // 2 + 1], (8, 128))
                shift = ((part - source) * 16) % 128
                if shift:
                    line = pltpu.roll(line, shift, 1)
                joined = jnp.where(group == part, line, joined)
            pieces.append(joined)
    for piece in range(8):
        wanted = jnp.broadcast_to(pieces[piece][0:1], (1024, 128))
        onehot[:, piece * 128 : piece * 128 + 128] = jnp.where(
            iota((1024, 128), 0) == wanted, 1.0, 0.0
        ).astype(BF16)
    loads[3].wait()
    for block in range(4):
        chosen[:, block * 256 : block * 256 + 256] = jnp.dot(
            leg[...], onehot[:, block * 256 : block * 256 + 256], preferred_element_type=F32
        ).astype(BF16)

    def sender_mode(r):
        d, e = r >> 3, (r >> 1) & 3
        return mode_of((x - (d >> 2)) & 3, (zh + (e >> 1)) & 1, (y - (d & 3)) & 3, (c + e) & 1)

    row, col = iota((128, 128), 0), iota((128, 128), 1)
    fine = cosine((first + sender_mode(row)) * col + (row & 1) * (NPHI // 4), NPHI)
    fine_hi, fine_lo = split(fine * (1.0 / math.sqrt(128.0)))
    row, col = iota((32, 128), 0), iota((32, 128), 1)
    turns = (first + sender_mode(col)) * row
    coarse_cos = cosine(turns, 32)
    coarse_sin = cosine(turns + 8 - 16 * (col & 1), 32)

    loads[2].wait()
    weight8 = counts[...].astype(F32) * (0.125 / math.sqrt(NT))
    weight = jnp.concatenate([weight8[i : i + 1] for i in range(8)], axis=1)

    total = a_send[0]
    for d in range(1, 16):
        a_copies[d - 1].wait_recv()
        total = total + a_recv[d]

    b_copies = []
    for e in range(1, 4):
        b_send[e] = total[2 * e : 2 * e + 2]
        b_copies.append(send(b_send.at[e], b_recv.at[e], b_ssem.at[e], b_rsem.at[e], column(0, e)))
    modes = total[0:2]
    for e in range(1, 4):
        b_copies[e - 1].wait_recv()
        modes = modes + b_recv[e]
    modes = modes * weight

    zeros = jnp.zeros((14, 1024), F32)
    direct = jnp.concatenate([modes, zeros], axis=0).astype(BF16)
    crossed = jnp.concatenate([modes[1:2], -modes[0:1], zeros], axis=0).astype(BF16)
    loads[4].wait()
    over_b = (((1,), (1,)), ((), ()))
    alm = lax.dot_general(direct, beam[0], over_b, preferred_element_type=F32)
    alm = alm + lax.dot_general(crossed, beam[1], over_b, preferred_element_type=F32)
    cycles = jnp.dot(alm.astype(BF16), chosen[...], preferred_element_type=F32)

    for block in range(4):
        c_send[block] = cycles[0:2, block * 256 : block * 256 + 256]
    c_copies = []
    for q in range(1, 16):
        e = q % 4
        block = ((zh + e // 2) % 2) * 2 + (c + e % 2) % 2
        c_copies.append(
            send(c_send.at[block], c_recv.at[q], c_ssem.at[q], c_rsem.at[q], column(q // 4, e))
        )
    mine = c_send[zh * 2 + c]
    sums = []
    for e in range(4):
        summed = mine
        for df in range(4):
            q = df * 4 + e
            if q:
                c_copies[q - 1].wait_recv()
            if df == 0:
                summed = c_recv[q] if q else mine
            else:
                summed = summed + c_recv[q]
        sums.append(summed)
    gathered = jnp.concatenate(sums, axis=0)
    d_send[0] = gathered[:, 0:128]
    d_send[1] = gathered[:, 128:256]

    d_copies = []
    for d in range(1, 16):
        half = ((x + d // 4) % 4) // 2
        d_copies.append(send(d_send.at[half], d_recv.at[d], d_ssem.at[d], d_rsem.at[d], plane(d)))
    d_recv[0] = d_send[x // 2]
    for copy in d_copies:
        copy.wait_recv()
    turned[...] = d_recv[...].reshape(128, 128).T
    place = (x % 2) * 4 + y
    values = turned[pl.ds(pl.multiple_of(place * 16, 16), 16), :]
    odd = (iota((16, 128), 1) & 1) == 1
    swapped = jnp.where(odd, pltpu.roll(values, 1, 1), pltpu.roll(values, 127, 1))
    moved = jnp.concatenate(
        [values * coarse_cos[a : a + 1] + swapped * coarse_sin[a : a + 1] for a in range(32)], axis=0
    )
    moved_hi, moved_lo = split(moved)
    image = jnp.dot(moved_hi, fine_hi, preferred_element_type=F32)
    image = image + jnp.dot(moved_lo, fine_hi, preferred_element_type=F32)
    image = image + jnp.dot(moved_hi, fine_lo, preferred_element_type=F32)
    for a in range(32):
        out_ref[:, a * 128 : a * 128 + 128] = image[a * 16 : a * 16 + 16]

    for copy in a_copies + b_copies + c_copies + d_copies:
        copy.wait_send()


def local(vis, counts, band_start, beam, legendre, cycle_index):
    anywhere = pl.BlockSpec(memory_space=pl.ANY)
    dma = pltpu.SemaphoreType.DMA
    return pl.pallas_call(
        body,
        out_shape=jax.ShapeDtypeStruct((16, NPHI), F32),
        in_specs=[
            anywhere,
            anywhere,
            pl.BlockSpec(memory_space=pltpu.SMEM),
            anywhere,
            anywhere,
            anywhere,
        ],
        out_specs=pl.BlockSpec(memory_space=pltpu.VMEM),
        scratch_shapes=[
            pltpu.VMEM((2, 32, 1024), F32),
            pltpu.VMEM((8, 128), I32),
            pltpu.VMEM((2, 1024, 1024), BF16),
            pltpu.VMEM((1024, 1024), BF16),
            pltpu.VMEM((8, 128), I32),
            pltpu.VMEM((1024, 1024), BF16),
            pltpu.VMEM((1024, 1024), BF16),
            pltpu.VMEM((16, 8, 1024), F32),
            pltpu.VMEM((16, 8, 1024), F32),
            pltpu.VMEM((4, 2, 1024), F32),
            pltpu.VMEM((4, 2, 1024), F32),
            pltpu.VMEM((4, 2, 256), F32),
            pltpu.VMEM((16, 2, 256), F32),
            pltpu.VMEM((2, 8, 128), F32),
            pltpu.VMEM((16, 8, 128), F32),
            pltpu.VMEM((128, 128), F32),
            dma((5,)),
            dma((16,)),
            dma((16,)),
            dma((4,)),
            dma((4,)),
            dma((16,)),
            dma((16,)),
            dma((16,)),
            dma((16,)),
        ],
        compiler_params=pltpu.CompilerParams(
            collective_id=0, has_side_effects=True, vmem_limit_bytes=56 * 1024 * 1024
        ),
    )(
        vis,
        counts.reshape(8, 128),
        band_start,
        beam,
        legendre,
        cycle_index.reshape(8, 128),
    )


def solution(mesh):
    return jax.shard_map(
        local,
        mesh=mesh,
        in_specs=(
            P("freq", None, "shard", None),
            P(),
            P(),
            P("freq", "shard", None, None, None),
            P("shard", None, None),
            P(),
        ),
        out_specs=P("shard", None),
        check_vma=False,
    )
```

```python
import functools
import math

import jax
import jax.numpy as jnp
from jax import lax
from jax.experimental import pallas as pl
from jax.experimental.pallas import tpu as pltpu
from jax.sharding import PartitionSpec as P

NT = 2048
NPHI = 4096
F32 = jnp.float32
BF16 = jnp.bfloat16
I32 = jnp.int32


def iota(shape, axis):
    return lax.broadcasted_iota(I32, shape, axis)


def cosine(turns, length):
    half = length // 2
    folded = ((turns + half) & (length - 1)) - half
    x = (length // 4 - jnp.abs(folded)).astype(F32) * (2.0 * math.pi / length)
    square = x * x
    total = jnp.full_like(x, 1.0 / math.factorial(13))
    for power, sign in ((11, -1), (9, 1), (7, -1), (5, 1), (3, -1), (1, 1)):
        total = total * square + sign / math.factorial(power)
    return total * x


def split(value):
    high = value.astype(BF16)
    return high, (value - high.astype(F32)).astype(BF16)


def hops(d):
    return min(d // 4, 4 - d // 4) + min(d % 4, 4 - d % 4)


FAR_FIRST = sorted(range(1, 16), key=hops, reverse=True)
COLUMN = [q for q in range(1, 16) if q % 4 >= 2] + [q for q in range(1, 16) if q % 4 < 2]


def mode_of(x, zh, y, c):
    return ((x * 2 + zh) * 4 + y) * 2 + c


def body(
    vis_hbm,
    counts_hbm,
    band_hbm,
    beam_hbm,
    leg_hbm,
    index_hbm,
    out_ref,
    vis,
    swapped_vis,
    counts,
    band,
    beam,
    leg,
    index,
    onehot,
    chosen,
    a_send,
    a_recv,
    b_send,
    b_recv,
    c_send,
    c_recv,
    d_send,
    d_recv,
    turned,
    load_sem,
    core_sem,
    a_ssem,
    a_rsem,
    b_ssem,
    b_rsem,
    c_ssem,
    c_rsem,
    d_ssem,
    d_rsem,
):
    f = lax.axis_index("freq")
    s = lax.axis_index("shard")
    x, zh, y, c = s // 16, (s // 8) % 2, (s // 2) % 4, s % 2

    def shard_of(px, pz, py, pc):
        return ((px * 2 + pz) * 4 + py) * 2 + pc

    def plane(d):
        return f, shard_of((x + d // 4) % 4, zh, (y + d % 4) % 4, c)

    def column(df, e):
        return (f + df) % 4, shard_of(x, (zh + e // 2) % 2, y, (c + e % 2) % 2)

    barrier = pltpu.get_barrier_semaphore()
    partners = [plane(d) for d in range(1, 16)]
    partners += [column(q // 4, q % 4) for q in range(1, 16)]
    for partner in partners:
        pl.semaphore_signal(
            barrier, inc=1, device_id=partner, device_id_type=pl.DeviceIdType.MESH
        )

    def load(src, dst, i):
        copy = pltpu.make_async_copy(src, dst, load_sem.at[i])
        copy.start()
        return copy

    band_load = load(band_hbm, band, 6)
    loads = [
        load(vis_hbm.at[0, :, :, 0:512], vis.at[0], 0),
        load(vis_hbm.at[0, :, :, 512:1024], vis.at[1], 5),
        load(index_hbm, index, 1),
        load(counts_hbm, counts, 2),
        load(leg_hbm.at[0], leg, 3),
        load(beam_hbm.at[0, 0], beam, 4),
    ]

    band_load.wait()
    first = band[0]

    row, col = iota((128, 256), 0), iota((128, 256), 1)
    d, e, ri = row >> 3, (row >> 1) & 3, row & 1
    k = mode_of((x + (d >> 2)) & 3, (zh + (e >> 1)) & 1, (y + (d & 3)) & 3, (c + e) & 1)
    quarter = (ri - ((col >> 5) & 1)) * (NT // 4)
    low_part = ((col >> 6) & 1) == 1

    def time_table(core):
        time = ((s // 2) * 2 + core) * 32 + (col & 31)
        high, low = split(cosine((first + k) * time + quarter, NT))
        return jnp.where(low_part, low.astype(F32), high.astype(F32)).astype(BF16)

    def spectrum(table, samples):
        high, low = split(samples.reshape(64, 512))
        stream = jnp.concatenate([high, high, low, low], axis=0)
        return jnp.dot(table, stream, preferred_element_type=F32)

    own_table, other_table = time_table(c), time_table(1 - c)
    loads[0].wait()
    loads[1].wait()
    pl.semaphore_wait(barrier, 30)

    def send(src, dst, ssem, rsem, target):
        copy = pltpu.make_async_remote_copy(
            src_ref=src,
            dst_ref=dst,
            send_sem=ssem,
            recv_sem=rsem,
            device_id=target,
            device_id_type=pl.DeviceIdType.MESH,
        )
        copy.start()
        return copy

    swap = send(vis.at[1 - c], swapped_vis, core_sem.at[0], core_sem.at[1], (f, s + 1 - 2 * c))
    partial = spectrum(own_table, vis[c])
    swap.wait_recv()
    partial = partial + spectrum(other_table, swapped_vis[...])
    a_send[...] = partial.reshape(16, 8, 512)

    a_copies = [
        send(a_send.at[d], a_recv.at[d], a_ssem.at[d], a_rsem.at[d], plane(d))
        for d in FAR_FIRST
    ]

    loads[2].wait()
    stored = index[...]
    lane = iota((8, 128), 1)
    group = lane >> 4
    pieces = []
    for block in range(4):
        for half in range(2):
            joined = jnp.zeros((8, 128), I32)
            for part in range(8):
                px, py = half * 2 + part // 4, part % 4
                source = py * 2 + block % 2
                line = jnp.broadcast_to(stored[px * 2 + block // 2 : px * 2 + block // 2 + 1], (8, 128))
                shift = ((part - source) * 16) % 128
                if shift:
                    line = pltpu.roll(line, shift, 1)
                joined = jnp.where(group == part, line, joined)
            pieces.append(joined)
    for piece in range(8):
        wanted = jnp.broadcast_to(pieces[piece][0:1], (1024, 128))
        onehot[:, piece * 128 : piece * 128 + 128] = jnp.where(
            iota((1024, 128), 0) == wanted, 1.0, 0.0
        ).astype(BF16)
    loads[4].wait()
    for block in range(4):
        chosen[:, block * 256 : block * 256 + 256] = jnp.dot(
            leg[...], onehot[:, block * 256 : block * 256 + 256], preferred_element_type=F32
        ).astype(BF16)

    loads[3].wait()
    weight8 = counts[...].astype(F32) * (0.125 / math.sqrt(NT))
    weight = jnp.concatenate([weight8[i : i + 1] for i in range(8)], axis=1)

    total = a_send[0]
    for d, copy in reversed(list(zip(FAR_FIRST, a_copies))):
        copy.wait_recv()
        total = total + a_recv[d]

    b_copies = []
    for e in (2, 3, 1):
        b_send[e] = total[2 * e : 2 * e + 2]
        b_copies.append(send(b_send.at[e], b_recv.at[e], b_ssem.at[e], b_rsem.at[e], column(0, e)))
    for copy in b_copies:
        copy.wait_recv()
    near = total[0:2] + b_recv[2]
    far = b_recv[1] + b_recv[3]
    modes = jnp.concatenate(
        [jnp.where(c == 0, near, far), jnp.where(c == 0, far, near)], axis=1
    )
    modes = modes * weight

    zeros = jnp.zeros((14, 1024), F32)
    direct = jnp.concatenate([modes, zeros], axis=0).astype(BF16)
    crossed = jnp.concatenate([modes[1:2], -modes[0:1], zeros], axis=0).astype(BF16)
    loads[5].wait()
    over_b = (((1,), (1,)), ((), ()))
    alm = lax.dot_general(direct, beam[0], over_b, preferred_element_type=F32)
    alm = alm + lax.dot_general(crossed, beam[1], over_b, preferred_element_type=F32)
    cycles = jnp.dot(alm.astype(BF16), chosen[...], preferred_element_type=F32)

    for block in range(4):
        c_send[block] = cycles[0:2, block * 256 : block * 256 + 256]
    c_copies = {}
    for q in COLUMN:
        e = q % 4
        block = ((zh + e // 2) % 2) * 2 + (c + e % 2) % 2
        c_copies[q] = send(
            c_send.at[block], c_recv.at[q], c_ssem.at[q], c_rsem.at[q], column(q // 4, e)
        )
    mine = c_send[zh * 2 + c]
    sums = []
    for e in range(4):
        summed = mine
        for df in range(4):
            q = df * 4 + e
            if q:
                c_copies[q].wait_recv()
            if df == 0:
                summed = c_recv[q] if q else mine
            else:
                summed = summed + c_recv[q]
        sums.append(summed)
    gathered = jnp.concatenate(sums, axis=0)
    d_send[0] = gathered[:, 0:128]
    d_send[1] = gathered[:, 128:256]

    d_copies = []
    for d in FAR_FIRST:
        half = ((x + d // 4) % 4) // 2
        d_copies.append(send(d_send.at[half], d_recv.at[d], d_ssem.at[d], d_rsem.at[d], plane(d)))
    d_recv[0] = d_send[x // 2]
    for copy in d_copies:
        copy.wait_recv()
    turned[...] = d_recv[...].reshape(128, 128).T
    place = (x % 2) * 4 + y
    values = turned[pl.ds(pl.multiple_of(place * 16, 16), 16), :]
    out_ref[...] = values
    for copy in [swap] + a_copies + b_copies + list(c_copies.values()) + d_copies:
        copy.wait_send()


def paint(band_hbm, values_hbm, out_hbm, band, values_ref, pieces, sem):
    band_load = pltpu.make_async_copy(band_hbm, band, sem.at[0])
    band_load.start()
    values_load = pltpu.make_async_copy(values_hbm, values_ref, sem.at[1])
    values_load.start()
    band_load.wait()
    first = band[0]
    s = lax.axis_index("shard")
    x, zh, y, c = s // 16, (s // 8) % 2, (s // 2) % 4, s % 2

    def sender_mode(r):
        d, e = r >> 3, (r >> 1) & 3
        return mode_of((x - (d >> 2)) & 3, (zh + (e >> 1)) & 1, (y - (d & 3)) & 3, (c + e) & 1)

    row, col = iota((128, 128), 0), iota((128, 128), 1)
    fine = cosine((first + sender_mode(row)) * col + (row & 1) * (NPHI // 4), NPHI)
    fine_hi, fine_lo = split(fine * (1.0 / math.sqrt(128.0)))
    row, col = iota((32, 128), 0), iota((32, 128), 1)
    turns = (first + sender_mode(col)) * row
    coarse_cos = cosine(turns, 32)
    coarse_sin = cosine(turns + 8 - 16 * (col & 1), 32)

    values_load.wait()
    values = values_ref[...]
    odd = (iota((16, 128), 1) & 1) == 1
    swapped = jnp.where(odd, pltpu.roll(values, 1, 1), pltpu.roll(values, 127, 1))
    copies = []
    for piece in range(4):
        moved = jnp.concatenate(
            [
                values * coarse_cos[a : a + 1] + swapped * coarse_sin[a : a + 1]
                for a in range(piece * 8, piece * 8 + 8)
            ],
            axis=0,
        )
        moved_hi, moved_lo = split(moved)
        image = jnp.dot(moved_hi, fine_hi, preferred_element_type=F32)
        image = image + jnp.dot(moved_lo, fine_hi, preferred_element_type=F32)
        image = image + jnp.dot(moved_hi, fine_lo, preferred_element_type=F32)
        for a in range(8):
            pieces[piece, :, a * 128 : a * 128 + 128] = image[a * 16 : a * 16 + 16]
        copy = pltpu.make_async_copy(
            pieces.at[piece], out_hbm.at[:, piece * 1024 : piece * 1024 + 1024], sem.at[2 + piece]
        )
        copy.start()
        copies.append(copy)
    for copy in copies:
        copy.wait()


def local(vis, counts, band_start, beam, legendre, cycle_index):
    anywhere = pl.BlockSpec(memory_space=pl.ANY)
    dma = pltpu.SemaphoreType.DMA
    values = pl.pallas_call(
        body,
        out_shape=jax.ShapeDtypeStruct((16, 128), F32),
        in_specs=[
            anywhere,
            anywhere,
            anywhere,
            anywhere,
            anywhere,
            anywhere,
        ],
        out_specs=pl.BlockSpec(memory_space=pltpu.VMEM),
        scratch_shapes=[
            pltpu.VMEM((2, 2, 32, 512), F32),
            pltpu.VMEM((2, 32, 512), F32),
            pltpu.VMEM((8, 128), I32),
            pltpu.SMEM((1,), I32),
            pltpu.VMEM((2, 1024, 1024), BF16),
            pltpu.VMEM((1024, 1024), BF16),
            pltpu.VMEM((8, 128), I32),
            pltpu.VMEM((1024, 1024), BF16),
            pltpu.VMEM((1024, 1024), BF16),
            pltpu.VMEM((16, 8, 512), F32),
            pltpu.VMEM((16, 8, 512), F32),
            pltpu.VMEM((4, 2, 512), F32),
            pltpu.VMEM((4, 2, 512), F32),
            pltpu.VMEM((4, 2, 256), F32),
            pltpu.VMEM((16, 2, 256), F32),
            pltpu.VMEM((2, 8, 128), F32),
            pltpu.VMEM((16, 8, 128), F32),
            pltpu.VMEM((128, 128), F32),
            dma((7,)),
            dma((2,)),
            dma((16,)),
            dma((16,)),
            dma((4,)),
            dma((4,)),
            dma((16,)),
            dma((16,)),
            dma((16,)),
            dma((16,)),
        ],
        compiler_params=pltpu.CompilerParams(
            collective_id=0, has_side_effects=True, vmem_limit_bytes=56 * 1024 * 1024
        ),
    )(
        vis,
        counts.reshape(8, 128),
        band_start,
        beam,
        legendre,
        cycle_index.reshape(8, 128),
    )
    return pl.pallas_call(
        paint,
        out_shape=jax.ShapeDtypeStruct((16, NPHI), F32),
        in_specs=[anywhere, anywhere],
        out_specs=anywhere,
        scratch_shapes=[
            pltpu.SMEM((1,), I32),
            pltpu.VMEM((16, 128), F32),
            pltpu.VMEM((4, 16, 1024), F32),
            dma((6,)),
        ],
    )(band_start, values)


def solution(mesh):
    return jax.shard_map(
        local,
        mesh=mesh,
        in_specs=(
            P("freq", None, "shard", None),
            P(),
            P(),
            P("freq", "shard", None, None, None),
            P("shard", None, None),
            P(),
        ),
        out_specs=P("shard", None),
        check_vma=False,
    )
```

```python
import functools
import math

import jax
import jax.numpy as jnp
from jax import lax
from jax.experimental import pallas as pl
from jax.experimental.pallas import tpu as pltpu
from jax.sharding import PartitionSpec as P

NT = 2048
NPHI = 4096
F32 = jnp.float32
BF16 = jnp.bfloat16
I32 = jnp.int32


def iota(shape, axis):
    return lax.broadcasted_iota(I32, shape, axis)


def cosine(turns, length):
    half = length // 2
    folded = ((turns + half) & (length - 1)) - half
    x = (length // 4 - jnp.abs(folded)).astype(F32) * (2.0 * math.pi / length)
    square = x * x
    total = jnp.full_like(x, 1.0 / math.factorial(13))
    for power, sign in ((11, -1), (9, 1), (7, -1), (5, 1), (3, -1), (1, 1)):
        total = total * square + sign / math.factorial(power)
    return total * x


def split(value):
    high = value.astype(BF16)
    return high, (value - high.astype(F32)).astype(BF16)


def hops(d):
    return min(d // 4, 4 - d // 4) + min(d % 4, 4 - d % 4)


FAR_FIRST = sorted(range(1, 16), key=hops, reverse=True)
COLUMN = [q for q in range(1, 16) if q % 4 >= 2] + [q for q in range(1, 16) if q % 4 < 2]


def mode_of(x, zh, y, c):
    return ((x * 2 + zh) * 4 + y) * 2 + c


def body(
    vis_hbm,
    counts_hbm,
    band_hbm,
    beam_hbm,
    leg_hbm,
    index_hbm,
    out_ref,
    vis,
    counts,
    band,
    beam,
    leg,
    index,
    onehot,
    chosen,
    a_send,
    a_recv,
    step_send,
    step_recv,
    b_send,
    b_recv,
    c_send,
    c_recv,
    d_send,
    d_recv,
    turned,
    load_sem,
    a_ssem,
    a_rsem,
    step_ssem,
    step_rsem,
    b_ssem,
    b_rsem,
    c_ssem,
    c_rsem,
    d_ssem,
    d_rsem,
):
    f = lax.axis_index("freq")
    s = lax.axis_index("shard")
    x, zh, y, c = s // 16, (s // 8) % 2, (s // 2) % 4, s % 2

    def shard_of(px, pz, py, pc):
        return ((px * 2 + pz) * 4 + py) * 2 + pc

    def plane(d):
        return f, shard_of((x + d // 4) % 4, zh, (y + d % 4) % 4, c)

    def column(df, e):
        return (f + df) % 4, shard_of(x, (zh + e // 2) % 2, y, (c + e % 2) % 2)

    barrier = pltpu.get_barrier_semaphore()
    partners = [plane(d) for d in FAR_FIRST] + [column(q // 4, q % 4) for q in COLUMN]
    for partner in partners:
        pl.semaphore_signal(
            barrier, inc=1, device_id=partner, device_id_type=pl.DeviceIdType.MESH
        )

    def load(src, dst, i):
        copy = pltpu.make_async_copy(src, dst, load_sem.at[i])
        copy.start()
        return copy

    band_load = load(band_hbm, band, 6)
    loads = [
        load(vis_hbm.at[0], vis, 0),
        load(index_hbm, index, 1),
        load(counts_hbm, counts, 2),
        load(leg_hbm.at[0], leg, 3),
        load(beam_hbm.at[0, 0], beam, 4),
    ]

    band_load.wait()
    first = band[0]

    row, col = iota((128, 256), 0), iota((128, 256), 1)
    d, e, ri = row >> 3, (row >> 1) & 3, row & 1
    k = mode_of((x + (d >> 2)) & 3, (zh + (e >> 1)) & 1, (y + (d & 3)) & 3, (c + e) & 1)
    quarter = (ri - ((col >> 5) & 1)) * (NT // 4)
    table_hi, table_lo = split(cosine((first + k) * (s * 32 + (col & 31)) + quarter, NT))
    low_part = ((col >> 6) & 1) == 1
    table = jnp.where(low_part, table_lo.astype(F32), table_hi.astype(F32)).astype(BF16)
    loads[0].wait()
    vis_hi, vis_lo = split(vis[...].reshape(64, 1024))
    stream = jnp.concatenate([vis_hi, vis_hi, vis_lo, vis_lo], axis=0)
    partial = jnp.dot(table, stream, preferred_element_type=F32)

    for d in range(1, 16):
        part = partial[d * 8 : d * 8 + 8]
        part = jnp.concatenate([part[:, 0:512], part[:, 512:1024]], axis=0)
        largest = jnp.maximum(jnp.max(jnp.abs(part), axis=(0, 1), keepdims=True), 1e-30)
        a_send[d] = jnp.round(part * (32767.0 / largest)).astype(I32).astype(jnp.int16)
        step_send[d] = jnp.broadcast_to(largest * (1.0 / 32767.0), (1, 128))

    pl.semaphore_wait(barrier, 30)

    def send(src, dst, ssem, rsem, target):
        copy = pltpu.make_async_remote_copy(
            src_ref=src,
            dst_ref=dst,
            send_sem=ssem,
            recv_sem=rsem,
            device_id=target,
            device_id_type=pl.DeviceIdType.MESH,
        )
        copy.start()
        return copy

    step_copies = [
        send(step_send.at[d], step_recv.at[d], step_ssem.at[d], step_rsem.at[d], plane(d))
        for d in FAR_FIRST
    ]
    a_copies = [
        send(a_send.at[d], a_recv.at[d], a_ssem.at[d], a_rsem.at[d], plane(d))
        for d in FAR_FIRST
    ]

    loads[1].wait()
    stored = index[...]
    lane = iota((8, 128), 1)
    group = lane >> 4
    pieces = []
    for block in range(4):
        for half in range(2):
            joined = jnp.zeros((8, 128), I32)
            for part in range(8):
                px, py = half * 2 + part // 4, part % 4
                source = py * 2 + block % 2
                line = jnp.broadcast_to(stored[px * 2 + block // 2 : px * 2 + block // 2 + 1], (8, 128))
                shift = ((part - source) * 16) % 128
                if shift:
                    line = pltpu.roll(line, shift, 1)
                joined = jnp.where(group == part, line, joined)
            pieces.append(joined)
    for piece in range(8):
        wanted = jnp.broadcast_to(pieces[piece][0:1], (1024, 128))
        onehot[:, piece * 128 : piece * 128 + 128] = jnp.where(
            iota((1024, 128), 0) == wanted, 1.0, 0.0
        ).astype(BF16)
    loads[3].wait()
    for block in range(4):
        chosen[:, block * 256 : block * 256 + 256] = jnp.dot(
            leg[...], onehot[:, block * 256 : block * 256 + 256], preferred_element_type=F32
        ).astype(BF16)

    def sender_mode(r):
        d, e = r >> 3, (r >> 1) & 3
        return mode_of((x - (d >> 2)) & 3, (zh + (e >> 1)) & 1, (y - (d & 3)) & 3, (c + e) & 1)

    row, col = iota((128, 128), 0), iota((128, 128), 1)
    fine = cosine((first + sender_mode(row)) * col + (row & 1) * (NPHI // 4), NPHI)
    fine_hi, fine_lo = split(fine * (1.0 / math.sqrt(128.0)))
    row, col = iota((32, 128), 0), iota((32, 128), 1)
    turns = (first + sender_mode(col)) * row
    coarse_cos = cosine(turns, 32)
    coarse_sin = cosine(turns + 8 - 16 * (col & 1), 32)

    loads[2].wait()
    weight8 = counts[...].astype(F32) * (0.125 / math.sqrt(NT))
    weight = jnp.concatenate([weight8[i : i + 1] for i in range(8)], axis=1)

    total = jnp.concatenate([partial[0:8, 0:512], partial[0:8, 512:1024]], axis=0)
    for d, step_copy, copy in reversed(list(zip(FAR_FIRST, step_copies, a_copies))):
        step_copy.wait_recv()
        copy.wait_recv()
        step = jnp.concatenate([step_recv[d]] * 4, axis=1)
        total = total + a_recv[d].astype(I32).astype(F32) * step
    total = jnp.concatenate([total[0:8], total[8:16]], axis=1)

    b_copies = []
    for e in (2, 3, 1):
        b_send[e] = total[2 * e : 2 * e + 2]
        b_copies.append(send(b_send.at[e], b_recv.at[e], b_ssem.at[e], b_rsem.at[e], column(0, e)))
    for copy in b_copies:
        copy.wait_recv()
    modes = total[0:2] + b_recv[1] + b_recv[2] + b_recv[3]
    modes = modes * weight

    zeros = jnp.zeros((14, 1024), F32)
    direct = jnp.concatenate([modes, zeros], axis=0).astype(BF16)
    crossed = jnp.concatenate([modes[1:2], -modes[0:1], zeros], axis=0).astype(BF16)
    loads[4].wait()
    over_b = (((1,), (1,)), ((), ()))
    alm = lax.dot_general(direct, beam[0], over_b, preferred_element_type=F32)
    alm = alm + lax.dot_general(crossed, beam[1], over_b, preferred_element_type=F32)
    cycles = jnp.dot(alm.astype(BF16), chosen[...], preferred_element_type=F32)

    for block in range(4):
        c_send[block] = cycles[0:2, block * 256 : block * 256 + 256]
    c_copies = {}
    for q in COLUMN:
        e = q % 4
        block = ((zh + e // 2) % 2) * 2 + (c + e % 2) % 2
        c_copies[q] = send(
            c_send.at[block], c_recv.at[q], c_ssem.at[q], c_rsem.at[q], column(q // 4, e)
        )
    mine = c_send[zh * 2 + c]
    sums = []
    for e in range(4):
        summed = mine
        for df in range(4):
            q = df * 4 + e
            if q:
                c_copies[q].wait_recv()
            if df == 0:
                summed = c_recv[q] if q else mine
            else:
                summed = summed + c_recv[q]
        sums.append(summed)
    gathered = jnp.concatenate(sums, axis=0)
    d_send[0] = gathered[:, 0:128]
    d_send[1] = gathered[:, 128:256]

    d_copies = []
    for d in FAR_FIRST:
        half = ((x + d // 4) % 4) // 2
        d_copies.append(send(d_send.at[half], d_recv.at[d], d_ssem.at[d], d_rsem.at[d], plane(d)))
    d_recv[0] = d_send[x // 2]
    for copy in d_copies:
        copy.wait_recv()
    turned[...] = d_recv[...].reshape(128, 128).T
    place = (x % 2) * 4 + y
    values = turned[pl.ds(pl.multiple_of(place * 16, 16), 16), :]
    odd = (iota((16, 128), 1) & 1) == 1
    swapped = jnp.where(odd, pltpu.roll(values, 1, 1), pltpu.roll(values, 127, 1))
    moved = jnp.concatenate(
        [values * coarse_cos[a : a + 1] + swapped * coarse_sin[a : a + 1] for a in range(32)], axis=0
    )
    moved_hi, moved_lo = split(moved)
    image = jnp.dot(moved_hi, fine_hi, preferred_element_type=F32)
    image = image + jnp.dot(moved_lo, fine_hi, preferred_element_type=F32)
    image = image + jnp.dot(moved_hi, fine_lo, preferred_element_type=F32)
    for a in range(32):
        out_ref[:, a * 128 : a * 128 + 128] = image[a * 16 : a * 16 + 16]

    for copy in step_copies + a_copies + b_copies + list(c_copies.values()) + d_copies:
        copy.wait_send()


def local(vis, counts, band_start, beam, legendre, cycle_index):
    anywhere = pl.BlockSpec(memory_space=pl.ANY)
    dma = pltpu.SemaphoreType.DMA
    return pl.pallas_call(
        body,
        out_shape=pltpu.VMEM((16, NPHI), F32),
        in_specs=[
            anywhere,
            anywhere,
            anywhere,
            anywhere,
            anywhere,
            anywhere,
        ],
        out_specs=pl.BlockSpec(memory_space=pltpu.VMEM),
        scratch_shapes=[
            pltpu.VMEM((2, 32, 1024), F32),
            pltpu.VMEM((8, 128), I32),
            pltpu.SMEM((1,), I32),
            pltpu.VMEM((2, 1024, 1024), BF16),
            pltpu.VMEM((1024, 1024), BF16),
            pltpu.VMEM((8, 128), I32),
            pltpu.VMEM((1024, 1024), BF16),
            pltpu.VMEM((1024, 1024), BF16),
            pltpu.VMEM((16, 16, 512), jnp.int16),
            pltpu.VMEM((16, 16, 512), jnp.int16),
            pltpu.VMEM((16, 1, 128), F32),
            pltpu.VMEM((16, 1, 128), F32),
            pltpu.VMEM((4, 2, 1024), F32),
            pltpu.VMEM((4, 2, 1024), F32),
            pltpu.VMEM((4, 2, 256), F32),
            pltpu.VMEM((16, 2, 256), F32),
            pltpu.VMEM((2, 8, 128), F32),
            pltpu.VMEM((16, 8, 128), F32),
            pltpu.VMEM((128, 128), F32),
            dma((7,)),
            dma((16,)),
            dma((16,)),
            dma((16,)),
            dma((16,)),
            dma((4,)),
            dma((4,)),
            dma((16,)),
            dma((16,)),
            dma((16,)),
            dma((16,)),
        ],
        compiler_params=pltpu.CompilerParams(
            collective_id=0, has_side_effects=True, vmem_limit_bytes=56 * 1024 * 1024
        ),
    )(
        vis,
        counts.reshape(8, 128),
        band_start,
        beam,
        legendre,
        cycle_index.reshape(8, 128),
    )

def solution(mesh):
    return jax.shard_map(
        local,
        mesh=mesh,
        in_specs=(
            P("freq", None, "shard", None),
            P(),
            P(),
            P("freq", "shard", None, None, None),
            P("shard", None, None),
            P(),
        ),
        out_specs=P("shard", None),
        check_vma=False,
    )
```

```python
import functools
import math

import jax
import jax.numpy as jnp
from jax import lax
from jax.experimental import pallas as pl
from jax.experimental.pallas import tpu as pltpu
from jax.sharding import PartitionSpec as P

NT = 2048
NPHI = 4096
F32 = jnp.float32
BF16 = jnp.bfloat16
I32 = jnp.int32


def iota(shape, axis):
    return lax.broadcasted_iota(I32, shape, axis)


def cosine(turns, length):
    half = length // 2
    folded = ((turns + half) & (length - 1)) - half
    x = (length // 4 - jnp.abs(folded)).astype(F32) * (2.0 * math.pi / length)
    square = x * x
    total = jnp.full_like(x, 1.0 / math.factorial(13))
    for power, sign in ((11, -1), (9, 1), (7, -1), (5, 1), (3, -1), (1, 1)):
        total = total * square + sign / math.factorial(power)
    return total * x


def split(value):
    high = value.astype(BF16)
    return high, (value - high.astype(F32)).astype(BF16)


def hops(d):
    return min(d // 4, 4 - d // 4) + min(d % 4, 4 - d % 4)


FAR_FIRST = sorted(range(1, 16), key=hops, reverse=True)


def all_hops(d):
    freq = (0, 1, 2, 1)[d // 64]
    return hops(d // 16 % 4 * 4 + d // 2 % 4) + 4 * (d // 8 % 2) + freq * (1 - d // 8 % 2)


ALL_FAR_FIRST = sorted(range(1, 256), key=all_hops, reverse=True)
COLUMN = [q for q in range(1, 16) if q % 4 >= 2] + [q for q in range(1, 16) if q % 4 < 2]


def mode_of(x, zh, y, c):
    return ((x * 2 + zh) * 4 + y) * 2 + c


def body(
    vis_hbm,
    counts_hbm,
    band_hbm,
    beam_hbm,
    leg_hbm,
    index_hbm,
    out_ref,
    vis,
    counts,
    band,
    beam,
    leg,
    index,
    onehot,
    chosen,
    a_send,
    a_recv,
    step_send,
    step_recv,
    b_send,
    b_recv,
    c_send,
    c_recv,
    load_sem,
    a_ssem,
    a_rsem,
    step_ssem,
    step_rsem,
    b_ssem,
    b_rsem,
    c_ssem,
    c_rsem,
):
    f = lax.axis_index("freq")
    s = lax.axis_index("shard")
    x, zh, y, c = s // 16, (s // 8) % 2, (s // 2) % 4, s % 2

    def shard_of(px, pz, py, pc):
        return ((px * 2 + pz) * 4 + py) * 2 + pc

    def plane(d):
        return f, shard_of((x + d // 4) % 4, zh, (y + d % 4) % 4, c)

    def anyone(d):
        return (f + d // 64) % 4, shard_of(
            (x + d // 16 % 4) % 4, (zh + d // 8 % 2) % 2, (y + d // 2 % 4) % 4, (c + d % 2) % 2
        )

    def column(df, e):
        return (f + df) % 4, shard_of(x, (zh + e // 2) % 2, y, (c + e % 2) % 2)

    barrier = pltpu.get_barrier_semaphore()
    partners = [plane(d) for d in FAR_FIRST] + [column(q // 4, q % 4) for q in COLUMN]
    for partner in partners:
        pl.semaphore_signal(
            barrier, inc=1, device_id=partner, device_id_type=pl.DeviceIdType.MESH
        )

    def load(src, dst, i):
        copy = pltpu.make_async_copy(src, dst, load_sem.at[i])
        copy.start()
        return copy

    band_load = load(band_hbm, band, 6)
    loads = [
        load(vis_hbm.at[0], vis, 0),
        load(index_hbm, index, 1),
        load(counts_hbm, counts, 2),
        load(leg_hbm.at[0], leg, 3),
        load(beam_hbm.at[0, 0], beam, 4),
    ]

    band_load.wait()
    first = band[0]

    row, col = iota((128, 256), 0), iota((128, 256), 1)
    d, e, ri = row >> 3, (row >> 1) & 3, row & 1
    k = mode_of((x + (d >> 2)) & 3, (zh + (e >> 1)) & 1, (y + (d & 3)) & 3, (c + e) & 1)
    quarter = (ri - ((col >> 5) & 1)) * (NT // 4)
    table_hi, table_lo = split(cosine((first + k) * (s * 32 + (col & 31)) + quarter, NT))
    low_part = ((col >> 6) & 1) == 1
    table = jnp.where(low_part, table_lo.astype(F32), table_hi.astype(F32)).astype(BF16)
    loads[0].wait()
    vis_hi, vis_lo = split(vis[...].reshape(64, 1024))
    stream = jnp.concatenate([vis_hi, vis_hi, vis_lo, vis_lo], axis=0)
    partial = jnp.dot(table, stream, preferred_element_type=F32)

    for d in range(1, 16):
        part = partial[d * 8 : d * 8 + 8]
        part = jnp.concatenate([part[:, 0:512], part[:, 512:1024]], axis=0)
        largest = jnp.maximum(jnp.max(jnp.abs(part), axis=(0, 1), keepdims=True), 1e-30)
        a_send[d] = jnp.round(part * (32767.0 / largest)).astype(I32).astype(jnp.int16)
        step_send[d] = jnp.broadcast_to(largest * (1.0 / 32767.0), (1, 128))

    pl.semaphore_wait(barrier, 30)

    def send(src, dst, ssem, rsem, target):
        copy = pltpu.make_async_remote_copy(
            src_ref=src,
            dst_ref=dst,
            send_sem=ssem,
            recv_sem=rsem,
            device_id=target,
            device_id_type=pl.DeviceIdType.MESH,
        )
        copy.start()
        return copy

    step_copies = [
        send(step_send.at[d], step_recv.at[d], step_ssem.at[d], step_rsem.at[d], plane(d))
        for d in FAR_FIRST
    ]
    a_copies = [
        send(a_send.at[d], a_recv.at[d], a_ssem.at[d], a_rsem.at[d], plane(d))
        for d in FAR_FIRST
    ]

    loads[1].wait()
    stored = index[...]
    for piece in range(8):
        wanted = jnp.broadcast_to(stored[piece : piece + 1], (1024, 128))
        onehot[:, piece * 128 : piece * 128 + 128] = jnp.where(
            iota((1024, 128), 0) == wanted, 1.0, 0.0
        ).astype(BF16)
    loads[3].wait()
    for block in range(4):
        chosen[:, block * 256 : block * 256 + 256] = jnp.dot(
            leg[...], onehot[:, block * 256 : block * 256 + 256], preferred_element_type=F32
        ).astype(BF16)

    def sender_mode(lane):
        d = lane & 63
        return mode_of((x - (d >> 4)) & 3, (zh + (d >> 3)) & 1, (y - (d >> 1)) & 3, (c + d) & 1)

    row, col = iota((128, 128), 0), iota((128, 128), 1)
    fine = cosine((first + sender_mode(row)) * col + (row >> 6) * (NPHI // 4), NPHI)
    fine_hi, fine_lo = split(fine * (1.0 / math.sqrt(128.0)))
    row, col = iota((32, 128), 0), iota((32, 128), 1)
    turns = (first + sender_mode(col)) * row
    coarse_cos = cosine(turns, 32)
    coarse_sin = cosine(turns + 8 - 16 * (col >> 6), 32)

    loads[2].wait()
    weight8 = counts[...].astype(F32) * (0.125 / math.sqrt(NT))
    weight = jnp.concatenate([weight8[i : i + 1] for i in range(8)], axis=1)

    total = jnp.concatenate([partial[0:8, 0:512], partial[0:8, 512:1024]], axis=0)
    for d, step_copy, copy in reversed(list(zip(FAR_FIRST, step_copies, a_copies))):
        step_copy.wait_recv()
        copy.wait_recv()
        step = jnp.concatenate([step_recv[d]] * 4, axis=1)
        total = total + a_recv[d].astype(I32).astype(F32) * step
    total = jnp.concatenate([total[0:8], total[8:16]], axis=1)

    b_copies = []
    for e in (2, 3, 1):
        b_send[e] = total[2 * e : 2 * e + 2]
        b_copies.append(send(b_send.at[e], b_recv.at[e], b_ssem.at[e], b_rsem.at[e], column(0, e)))
    for copy in b_copies:
        copy.wait_recv()
    modes = total[0:2] + b_recv[1] + b_recv[2] + b_recv[3]
    modes = modes * weight

    zeros = jnp.zeros((14, 1024), F32)
    direct = jnp.concatenate([modes, zeros], axis=0).astype(BF16)
    crossed = jnp.concatenate([modes[1:2], -modes[0:1], zeros], axis=0).astype(BF16)
    loads[4].wait()
    over_b = (((1,), (1,)), ((), ()))
    alm = lax.dot_general(direct, beam[0], over_b, preferred_element_type=F32)
    alm = alm + lax.dot_general(crossed, beam[1], over_b, preferred_element_type=F32)
    cycles = jnp.dot(alm.astype(BF16), chosen[...], preferred_element_type=F32)

    real = jnp.concatenate([cycles[0:1, i * 128 : i * 128 + 128] for i in range(8)], axis=0)
    imag = jnp.concatenate([cycles[1:2, i * 128 : i * 128 + 128] for i in range(8)], axis=0)
    first_lanes = iota((8, 128), 1) < 16
    for b in range(8):
        left = pltpu.roll(real, (128 - 16 * b) % 128, 1) if b else real
        right = pltpu.roll(imag, (144 - 16 * b) % 128, 1) if b != 1 else imag
        c_send[b * 8 : b * 8 + 8] = jnp.where(first_lanes, left, right).reshape(8, 1, 128)

    def row_of(shard):
        return shard % 8 * 8 + shard // 8

    for d in ALL_FAR_FIRST:
        target = anyone(d)
        send(c_send.at[row_of(target[1])], c_recv.at[d], c_ssem, c_rsem, target)
    c_recv[0] = c_send[row_of(s)]
    pltpu.make_async_copy(c_recv.at[1:256], c_recv.at[1:256], c_rsem).wait()
    summed = c_recv[0:64] + c_recv[64:128] + c_recv[128:192] + c_recv[192:256]
    summed = jnp.concatenate([summed.reshape(64, 128), jnp.zeros((64, 128), F32)], axis=0).T
    values = summed[0:16] + pltpu.roll(summed[16:32], 64, 1)
    swapped = pltpu.roll(values, 64, 1)
    moved = jnp.concatenate(
        [values * coarse_cos[a : a + 1] + swapped * coarse_sin[a : a + 1] for a in range(32)], axis=0
    )
    moved_hi, moved_lo = split(moved)
    image = jnp.dot(moved_hi, fine_hi, preferred_element_type=F32)
    image = image + jnp.dot(moved_lo, fine_hi, preferred_element_type=F32)
    image = image + jnp.dot(moved_hi, fine_lo, preferred_element_type=F32)
    for a in range(32):
        out_ref[:, a * 128 : a * 128 + 128] = image[a * 16 : a * 16 + 16]

    for copy in step_copies + a_copies + b_copies:
        copy.wait_send()
    pltpu.make_async_copy(c_recv.at[1:256], c_recv.at[1:256], c_ssem).wait()


def local(vis, counts, band_start, beam, legendre, cycle_index):
    anywhere = pl.BlockSpec(memory_space=pl.ANY)
    dma = pltpu.SemaphoreType.DMA
    return pl.pallas_call(
        body,
        out_shape=pltpu.VMEM((16, NPHI), F32),
        in_specs=[
            anywhere,
            anywhere,
            anywhere,
            anywhere,
            anywhere,
            anywhere,
        ],
        out_specs=pl.BlockSpec(memory_space=pltpu.VMEM),
        scratch_shapes=[
            pltpu.VMEM((2, 32, 1024), F32),
            pltpu.VMEM((8, 128), I32),
            pltpu.SMEM((1,), I32),
            pltpu.VMEM((2, 1024, 1024), BF16),
            pltpu.VMEM((1024, 1024), BF16),
            pltpu.VMEM((8, 128), I32),
            pltpu.VMEM((1024, 1024), BF16),
            pltpu.VMEM((1024, 1024), BF16),
            pltpu.VMEM((16, 16, 512), jnp.int16),
            pltpu.VMEM((16, 16, 512), jnp.int16),
            pltpu.VMEM((16, 1, 128), F32),
            pltpu.VMEM((16, 1, 128), F32),
            pltpu.VMEM((4, 2, 1024), F32),
            pltpu.VMEM((4, 2, 1024), F32),
            pltpu.VMEM((64, 1, 128), F32),
            pltpu.VMEM((256, 1, 128), F32),
            dma((7,)),
            dma((16,)),
            dma((16,)),
            dma((16,)),
            dma((16,)),
            dma((4,)),
            dma((4,)),
            dma,
            dma,
        ],
        compiler_params=pltpu.CompilerParams(
            collective_id=0, has_side_effects=True, vmem_limit_bytes=56 * 1024 * 1024
        ),
    )(
        vis,
        counts.reshape(8, 128),
        band_start,
        beam,
        legendre,
        cycle_index.reshape(8, 128),
    )

def solution(mesh):
    return jax.shard_map(
        local,
        mesh=mesh,
        in_specs=(
            P("freq", None, "shard", None),
            P(),
            P(),
            P("freq", "shard", None, None, None),
            P("shard", None, None),
            P(),
        ),
        out_specs=P("shard", None),
        check_vma=False,
    )
```

```python
import functools
import math

import jax
import jax.numpy as jnp
from jax import lax
from jax.experimental import pallas as pl
from jax.experimental.pallas import tpu as pltpu
from jax.sharding import PartitionSpec as P

NT = 2048
NPHI = 4096
F32 = jnp.float32
BF16 = jnp.bfloat16
I32 = jnp.int32


def iota(shape, axis):
    return lax.broadcasted_iota(I32, shape, axis)


def cosine(turns, length):
    half = length // 2
    folded = ((turns + half) & (length - 1)) - half
    x = (length // 4 - jnp.abs(folded)).astype(F32) * (2.0 * math.pi / length)
    square = x * x
    total = jnp.full_like(x, 1.0 / math.factorial(13))
    for power, sign in ((11, -1), (9, 1), (7, -1), (5, 1), (3, -1), (1, 1)):
        total = total * square + sign / math.factorial(power)
    return total * x


def split(value):
    high = value.astype(BF16)
    return high, (value - high.astype(F32)).astype(BF16)


def hops(d):
    return min(d // 4, 4 - d // 4) + min(d % 4, 4 - d % 4)


FAR_FIRST = sorted(range(1, 16), key=hops, reverse=True)


def all_hops(d):
    freq = (0, 1, 2, 1)[d // 64]
    return hops(d // 16 % 4 * 4 + d // 2 % 4) + 4 * (d // 8 % 2) + freq * (1 - d // 8 % 2)


ALL_FAR_FIRST = sorted(range(1, 256), key=all_hops, reverse=True)
COLUMN = [q for q in range(1, 16) if q % 4 >= 2] + [q for q in range(1, 16) if q % 4 < 2]


def mode_of(x, zh, y, c):
    return ((x * 2 + zh) * 4 + y) * 2 + c


def body(
    vis_hbm,
    counts_hbm,
    band_hbm,
    beam_hbm,
    leg_hbm,
    index_hbm,
    out_ref,
    vis,
    counts,
    band,
    beam,
    leg,
    index,
    onehot,
    chosen,
    across,
    a_send,
    a_recv,
    step_send,
    step_recv,
    b_send,
    b_recv,
    c_send,
    c_recv,
    load_sem,
    a_ssem,
    a_rsem,
    step_ssem,
    step_rsem,
    b_ssem,
    b_rsem,
    c_ssem,
    c_rsem,
):
    f = lax.axis_index("freq")
    s = lax.axis_index("shard")
    x, zh, y, c = s // 16, (s // 8) % 2, (s // 2) % 4, s % 2

    def shard_of(px, pz, py, pc):
        return ((px * 2 + pz) * 4 + py) * 2 + pc

    def plane(d):
        return f, shard_of((x + d // 4) % 4, zh, (y + d % 4) % 4, c)

    def anyone(d):
        return (f + d // 64) % 4, shard_of(
            (x + d // 16 % 4) % 4, (zh + d // 8 % 2) % 2, (y + d // 2 % 4) % 4, (c + d % 2) % 2
        )

    def column(df, e):
        return (f + df) % 4, shard_of(x, (zh + e // 2) % 2, y, (c + e % 2) % 2)

    barrier = pltpu.get_barrier_semaphore()
    partners = [plane(d) for d in FAR_FIRST] + [column(q // 4, q % 4) for q in COLUMN]
    for partner in partners:
        pl.semaphore_signal(
            barrier, inc=1, device_id=partner, device_id_type=pl.DeviceIdType.MESH
        )

    def load(src, dst, i):
        copy = pltpu.make_async_copy(src, dst, load_sem.at[i])
        copy.start()
        return copy

    band_load = load(band_hbm, band, 6)
    loads = [
        load(vis_hbm.at[0], vis, 0),
        load(index_hbm, index, 1),
        load(counts_hbm, counts, 2),
        load(leg_hbm.at[0], leg, 3),
        load(beam_hbm.at[0, 0], beam, 4),
    ]

    band_load.wait()
    first = band[0]

    row, col = iota((128, 256), 0), iota((128, 256), 1)
    d, e, ri = row >> 3, (row >> 1) & 3, row & 1
    k = mode_of((x + (d >> 2)) & 3, (zh + (e >> 1)) & 1, (y + (d & 3)) & 3, (c + e) & 1)
    quarter = (ri - ((col >> 5) & 1)) * (NT // 4)
    table_hi, table_lo = split(cosine((first + k) * (s * 32 + (col & 31)) + quarter, NT))
    low_part = ((col >> 6) & 1) == 1
    table = jnp.where(low_part, table_lo.astype(F32), table_hi.astype(F32)).astype(BF16)
    loads[0].wait()
    vis_hi, vis_lo = split(vis[...].reshape(64, 1024))
    stream = jnp.concatenate([vis_hi, vis_hi, vis_lo, vis_lo], axis=0)
    partial = jnp.dot(table, stream, preferred_element_type=F32)

    for d in range(1, 16):
        part = partial[d * 8 : d * 8 + 8]
        part = jnp.concatenate([part[:, 0:512], part[:, 512:1024]], axis=0)
        largest = jnp.maximum(jnp.max(jnp.abs(part), axis=(0, 1), keepdims=True), 1e-30)
        a_send[d] = jnp.round(part * (32767.0 / largest)).astype(I32).astype(jnp.int16)
        step_send[d] = jnp.broadcast_to(largest * (1.0 / 32767.0), (1, 128))

    pl.semaphore_wait(barrier, 30)

    def send(src, dst, ssem, rsem, target):
        copy = pltpu.make_async_remote_copy(
            src_ref=src,
            dst_ref=dst,
            send_sem=ssem,
            recv_sem=rsem,
            device_id=target,
            device_id_type=pl.DeviceIdType.MESH,
        )
        copy.start()
        return copy

    step_copies = [
        send(step_send.at[d], step_recv.at[d], step_ssem.at[d], step_rsem.at[d], plane(d))
        for d in FAR_FIRST
    ]
    a_copies = [
        send(a_send.at[d], a_recv.at[d], a_ssem.at[d], a_rsem.at[d], plane(d))
        for d in FAR_FIRST
    ]

    loads[1].wait()
    stored = index[...]
    for piece in range(8):
        wanted = jnp.broadcast_to(stored[piece : piece + 1], (1024, 128))
        onehot[:, piece * 128 : piece * 128 + 128] = jnp.where(
            iota((1024, 128), 0) == wanted, 1.0, 0.0
        ).astype(BF16)
    loads[3].wait()
    for block in range(4):
        chosen[:, block * 256 : block * 256 + 256] = jnp.dot(
            leg[...], onehot[:, block * 256 : block * 256 + 256], preferred_element_type=F32
        ).astype(BF16)

    loads[4].wait()
    for part in range(2):
        for block in range(4):
            lanes = slice(block * 256, block * 256 + 256)
            across[part * 1024 + block * 256 : part * 1024 + block * 256 + 256, :] = beam[part, :, lanes].T

    def sender_mode(lane):
        d = lane & 63
        return mode_of((x - (d >> 4)) & 3, (zh + (d >> 3)) & 1, (y - (d >> 1)) & 3, (c + d) & 1)

    row, col = iota((128, 128), 0), iota((128, 128), 1)
    fine = cosine((first + sender_mode(row)) * col + (row >> 6) * (NPHI // 4), NPHI)
    fine_hi, fine_lo = split(fine * (1.0 / math.sqrt(128.0)))
    row, col = iota((32, 128), 0), iota((32, 128), 1)
    turns = (first + sender_mode(col)) * row
    coarse_cos = cosine(turns, 32)
    coarse_sin = cosine(turns + 8 - 16 * (col >> 6), 32)

    loads[2].wait()
    weight8 = counts[...].astype(F32) * (0.125 / math.sqrt(NT))
    weight = jnp.concatenate([weight8[i : i + 1] for i in range(8)], axis=1)

    total = jnp.concatenate([partial[0:8, 0:512], partial[0:8, 512:1024]], axis=0)
    for d, step_copy, copy in zip(FAR_FIRST, step_copies, a_copies):
        step_copy.wait_recv()
        copy.wait_recv()
        step = jnp.concatenate([step_recv[d]] * 4, axis=1)
        total = total + a_recv[d].astype(I32).astype(F32) * step
    total = jnp.concatenate([total[0:8], total[8:16]], axis=1)

    b_copies = []
    for e in (2, 3, 1):
        b_send[e] = total[2 * e : 2 * e + 2]
        b_copies.append(send(b_send.at[e], b_recv.at[e], b_ssem.at[e], b_rsem.at[e], column(0, e)))
    for copy in b_copies:
        copy.wait_recv()
    modes = total[0:2] + b_recv[1] + b_recv[2] + b_recv[3]
    modes = modes * weight

    zeros = jnp.zeros((14, 1024), F32)
    direct = jnp.concatenate([modes, zeros], axis=0).astype(BF16)
    crossed = jnp.concatenate([modes[1:2], -modes[0:1], zeros], axis=0).astype(BF16)
    both = jnp.concatenate([direct, crossed], axis=1)
    alm = jnp.dot(both, across[...], preferred_element_type=F32)
    cycles = jnp.dot(alm.astype(BF16), chosen[...], preferred_element_type=F32)

    real = jnp.concatenate([cycles[0:1, i * 128 : i * 128 + 128] for i in range(8)], axis=0)
    imag = jnp.concatenate([cycles[1:2, i * 128 : i * 128 + 128] for i in range(8)], axis=0)
    first_lanes = iota((8, 128), 1) < 16
    for b in range(8):
        left = pltpu.roll(real, (128 - 16 * b) % 128, 1) if b else real
        right = pltpu.roll(imag, (144 - 16 * b) % 128, 1) if b != 1 else imag
        c_send[b * 8 : b * 8 + 8] = jnp.where(first_lanes, left, right).reshape(8, 1, 128)

    def row_of(shard):
        return shard % 8 * 8 + shard // 8

    for d in ALL_FAR_FIRST:
        target = anyone(d)
        send(c_send.at[row_of(target[1])], c_recv.at[d : d + 1], c_ssem, c_rsem, target)
    c_recv[0:1] = c_send[row_of(s)]
    pltpu.make_async_copy(c_recv.at[1:256], c_recv.at[1:256], c_rsem).wait()
    summed = c_recv[0:64] + c_recv[64:128] + c_recv[128:192] + c_recv[192:256]
    summed = jnp.concatenate([summed, jnp.zeros((64, 128), F32)], axis=0).T
    values = summed[0:16] + pltpu.roll(summed[16:32], 64, 1)
    swapped = pltpu.roll(values, 64, 1)
    moved = jnp.concatenate(
        [values * coarse_cos[a : a + 1] + swapped * coarse_sin[a : a + 1] for a in range(32)], axis=0
    )
    moved_hi, moved_lo = split(moved)
    image = jnp.dot(moved_hi, fine_hi, preferred_element_type=F32)
    image = image + jnp.dot(moved_lo, fine_hi, preferred_element_type=F32)
    image = image + jnp.dot(moved_hi, fine_lo, preferred_element_type=F32)
    for a in range(32):
        out_ref[:, a * 128 : a * 128 + 128] = image[a * 16 : a * 16 + 16]

    for copy in step_copies + a_copies + b_copies:
        copy.wait_send()
    pltpu.make_async_copy(c_recv.at[1:256], c_recv.at[1:256], c_ssem).wait()


def local(vis, counts, band_start, beam, legendre, cycle_index):
    anywhere = pl.BlockSpec(memory_space=pl.ANY)
    dma = pltpu.SemaphoreType.DMA
    return pl.pallas_call(
        body,
        out_shape=pltpu.VMEM((16, NPHI), F32),
        in_specs=[
            anywhere,
            anywhere,
            anywhere,
            anywhere,
            anywhere,
            anywhere,
        ],
        out_specs=pl.BlockSpec(memory_space=pltpu.VMEM),
        scratch_shapes=[
            pltpu.VMEM((2, 32, 1024), F32),
            pltpu.VMEM((8, 128), I32),
            pltpu.SMEM((1,), I32),
            pltpu.VMEM((2, 1024, 1024), BF16),
            pltpu.VMEM((1024, 1024), BF16),
            pltpu.VMEM((8, 128), I32),
            pltpu.VMEM((1024, 1024), BF16),
            pltpu.VMEM((1024, 1024), BF16),
            pltpu.VMEM((2048, 1024), BF16),
            pltpu.VMEM((16, 16, 512), jnp.int16),
            pltpu.VMEM((16, 16, 512), jnp.int16),
            pltpu.VMEM((16, 1, 128), F32),
            pltpu.VMEM((16, 1, 128), F32),
            pltpu.VMEM((4, 2, 1024), F32),
            pltpu.VMEM((4, 2, 1024), F32),
            pltpu.VMEM((64, 1, 128), F32),
            pltpu.VMEM((256, 128), F32),
            dma((7,)),
            dma((16,)),
            dma((16,)),
            dma((16,)),
            dma((16,)),
            dma((4,)),
            dma((4,)),
            dma,
            dma,
        ],
        compiler_params=pltpu.CompilerParams(
            collective_id=0, has_side_effects=True, vmem_limit_bytes=56 * 1024 * 1024
        ),
    )(
        vis,
        counts.reshape(8, 128),
        band_start,
        beam,
        legendre,
        cycle_index.reshape(8, 128),
    )

def solution(mesh):
    return jax.shard_map(
        local,
        mesh=mesh,
        in_specs=(
            P("freq", None, "shard", None),
            P(),
            P(),
            P("freq", "shard", None, None, None),
            P("shard", None, None),
            P(),
        ),
        out_specs=P("shard", None),
        check_vma=False,
    )
```

```python
import functools
import math

import jax
import jax.numpy as jnp
from jax import lax
from jax.experimental import pallas as pl
from jax.experimental.pallas import tpu as pltpu
from jax.sharding import PartitionSpec as P

NT = 2048
NPHI = 4096
F32 = jnp.float32
BF16 = jnp.bfloat16
I32 = jnp.int32


def iota(shape, axis):
    return lax.broadcasted_iota(I32, shape, axis)


def cosine(turns, length):
    half = length // 2
    folded = ((turns + half) & (length - 1)) - half
    x = (length // 4 - jnp.abs(folded)).astype(F32) * (2.0 * math.pi / length)
    square = x * x
    total = jnp.full_like(x, 1.0 / math.factorial(13))
    for power, sign in ((11, -1), (9, 1), (7, -1), (5, 1), (3, -1), (1, 1)):
        total = total * square + sign / math.factorial(power)
    return total * x


def split(value):
    high = value.astype(BF16)
    return high, (value - high.astype(F32)).astype(BF16)


def hops(d):
    return min(d // 4, 4 - d // 4) + min(d % 4, 4 - d % 4)


FAR_FIRST = sorted(range(1, 16), key=hops, reverse=True)


def all_hops(d):
    freq = (0, 1, 2, 1)[d // 64]
    return hops(d // 16 % 4 * 4 + d // 2 % 4) + 4 * (d // 8 % 2) + freq * (1 - d // 8 % 2)


ALL_FAR_FIRST = sorted(range(1, 256), key=all_hops, reverse=True)
COLUMN = [q for q in range(1, 16) if q % 4 >= 2] + [q for q in range(1, 16) if q % 4 < 2]


def mode_of(x, zh, y, c):
    return ((x * 2 + zh) * 4 + y) * 2 + c


def body(
    vis_hbm,
    counts_hbm,
    band_hbm,
    beam_hbm,
    leg_hbm,
    index_hbm,
    out_ref,
    cos_ref,
    sin_ref,
    high_ref,
    low_ref,
    vis,
    counts,
    band,
    beam,
    leg,
    index,
    onehot,
    chosen,
    across,
    a_send,
    a_recv,
    step_send,
    step_recv,
    b_send,
    b_recv,
    c_send,
    c_recv,
    load_sem,
    a_ssem,
    a_rsem,
    step_ssem,
    step_rsem,
    b_ssem,
    b_rsem,
    c_ssem,
    c_rsem,
):
    f = lax.axis_index("freq")
    s = lax.axis_index("shard")
    x, zh, y, c = s // 16, (s // 8) % 2, (s // 2) % 4, s % 2

    def shard_of(px, pz, py, pc):
        return ((px * 2 + pz) * 4 + py) * 2 + pc

    def plane(d):
        return f, shard_of((x + d // 4) % 4, zh, (y + d % 4) % 4, c)

    def anyone(d):
        return (f + d // 64) % 4, shard_of(
            (x + d // 16 % 4) % 4, (zh + d // 8 % 2) % 2, (y + d // 2 % 4) % 4, (c + d % 2) % 2
        )

    def column(df, e):
        return (f + df) % 4, shard_of(x, (zh + e // 2) % 2, y, (c + e % 2) % 2)

    barrier = pltpu.get_barrier_semaphore()
    partners = [plane(d) for d in FAR_FIRST] + [column(q // 4, q % 4) for q in COLUMN]
    for partner in partners:
        pl.semaphore_signal(
            barrier, inc=1, device_id=partner, device_id_type=pl.DeviceIdType.MESH
        )

    def load(src, dst, i):
        copy = pltpu.make_async_copy(src, dst, load_sem.at[i])
        copy.start()
        return copy

    band_load = load(band_hbm, band, 6)
    loads = [
        load(vis_hbm.at[0], vis, 0),
        load(index_hbm, index, 1),
        load(counts_hbm, counts, 2),
        load(leg_hbm.at[0], leg, 3),
        load(beam_hbm.at[0, 0], beam, 4),
    ]

    band_load.wait()
    first = band[0]

    row, col = iota((128, 256), 0), iota((128, 256), 1)
    d, e, ri = row >> 3, (row >> 1) & 3, row & 1
    k = mode_of((x + (d >> 2)) & 3, (zh + (e >> 1)) & 1, (y + (d & 3)) & 3, (c + e) & 1)
    quarter = (ri - ((col >> 5) & 1)) * (NT // 4)
    table_hi, table_lo = split(cosine((first + k) * (s * 32 + (col & 31)) + quarter, NT))
    low_part = ((col >> 6) & 1) == 1
    table = jnp.where(low_part, table_lo.astype(F32), table_hi.astype(F32)).astype(BF16)
    loads[0].wait()
    vis_hi, vis_lo = split(vis[...].reshape(64, 1024))
    stream = jnp.concatenate([vis_hi, vis_hi, vis_lo, vis_lo], axis=0)
    partial = jnp.dot(table, stream, preferred_element_type=F32)

    for d in range(1, 16):
        part = partial[d * 8 : d * 8 + 8]
        part = jnp.concatenate([part[:, 0:512], part[:, 512:1024]], axis=0)
        largest = jnp.maximum(jnp.max(jnp.abs(part), axis=(0, 1), keepdims=True), 1e-30)
        a_send[d] = jnp.round(part * (32767.0 / largest)).astype(I32).astype(jnp.int16)
        step_send[d] = jnp.broadcast_to(largest * (1.0 / 32767.0), (1, 128))

    pl.semaphore_wait(barrier, 30)

    def send(src, dst, ssem, rsem, target):
        copy = pltpu.make_async_remote_copy(
            src_ref=src,
            dst_ref=dst,
            send_sem=ssem,
            recv_sem=rsem,
            device_id=target,
            device_id_type=pl.DeviceIdType.MESH,
        )
        copy.start()
        return copy

    step_copies = [
        send(step_send.at[d], step_recv.at[d], step_ssem.at[d], step_rsem.at[d], plane(d))
        for d in FAR_FIRST
    ]
    a_copies = [
        send(a_send.at[d], a_recv.at[d], a_ssem.at[d], a_rsem.at[d], plane(d))
        for d in FAR_FIRST
    ]

    loads[1].wait()
    stored = index[...]
    for piece in range(8):
        wanted = jnp.broadcast_to(stored[piece : piece + 1], (1024, 128))
        onehot[:, piece * 128 : piece * 128 + 128] = jnp.where(
            iota((1024, 128), 0) == wanted, 1.0, 0.0
        ).astype(BF16)
    loads[3].wait()
    for block in range(4):
        chosen[:, block * 256 : block * 256 + 256] = jnp.dot(
            leg[...], onehot[:, block * 256 : block * 256 + 256], preferred_element_type=F32
        ).astype(BF16)

    loads[4].wait()
    for part in range(2):
        for block in range(4):
            lanes = slice(block * 256, block * 256 + 256)
            across[part * 1024 + block * 256 : part * 1024 + block * 256 + 256, :] = beam[part, :, lanes].T

    def sender_mode(lane):
        d = lane & 63
        return mode_of((x - (d >> 4)) & 3, (zh + (d >> 3)) & 1, (y - (d >> 1)) & 3, (c + d) & 1)

    row, col = iota((128, 128), 0), iota((128, 128), 1)
    fine = cosine((first + sender_mode(row)) * col + (row >> 6) * (NPHI // 4), NPHI)
    fine_hi, fine_lo = split(fine * (1.0 / math.sqrt(128.0)))
    row, col = iota((32, 128), 0), iota((32, 128), 1)
    turns = (first + sender_mode(col)) * row
    coarse_cos = cosine(turns, 32)
    coarse_sin = cosine(turns + 8 - 16 * (col >> 6), 32)

    cos_ref[...] = coarse_cos
    sin_ref[...] = coarse_sin
    high_ref[...] = fine_hi
    low_ref[...] = fine_lo

    loads[2].wait()
    weight8 = counts[...].astype(F32) * (0.125 / math.sqrt(NT))
    weight = jnp.concatenate([weight8[i : i + 1] for i in range(8)], axis=1)

    total = jnp.concatenate([partial[0:8, 0:512], partial[0:8, 512:1024]], axis=0)
    for d, step_copy, copy in zip(FAR_FIRST, step_copies, a_copies):
        step_copy.wait_recv()
        copy.wait_recv()
        step = jnp.concatenate([step_recv[d]] * 4, axis=1)
        total = total + a_recv[d].astype(I32).astype(F32) * step
    total = jnp.concatenate([total[0:8], total[8:16]], axis=1)

    b_copies = []
    for e in (2, 3, 1):
        b_send[e] = total[2 * e : 2 * e + 2]
        b_copies.append(send(b_send.at[e], b_recv.at[e], b_ssem.at[e], b_rsem.at[e], column(0, e)))
    for copy in b_copies:
        copy.wait_recv()
    modes = total[0:2] + b_recv[1] + b_recv[2] + b_recv[3]
    modes = modes * weight

    zeros = jnp.zeros((14, 1024), F32)
    direct = jnp.concatenate([modes, zeros], axis=0).astype(BF16)
    crossed = jnp.concatenate([modes[1:2], -modes[0:1], zeros], axis=0).astype(BF16)
    both = jnp.concatenate([direct, crossed], axis=1)
    alm = jnp.dot(both, across[...], preferred_element_type=F32)
    cycles = jnp.dot(alm.astype(BF16), chosen[...], preferred_element_type=F32)

    real = jnp.concatenate([cycles[0:1, i * 128 : i * 128 + 128] for i in range(8)], axis=0)
    imag = jnp.concatenate([cycles[1:2, i * 128 : i * 128 + 128] for i in range(8)], axis=0)
    first_lanes = iota((8, 128), 1) < 16
    for b in range(8):
        left = pltpu.roll(real, (128 - 16 * b) % 128, 1) if b else real
        right = pltpu.roll(imag, (144 - 16 * b) % 128, 1) if b != 1 else imag
        c_send[b * 8 : b * 8 + 8] = jnp.where(first_lanes, left, right).reshape(8, 1, 128)

    def row_of(shard):
        return shard % 8 * 8 + shard // 8

    for d in ALL_FAR_FIRST:
        target = anyone(d)
        send(c_send.at[row_of(target[1])], c_recv.at[d : d + 1], c_ssem, c_rsem, target)
    c_recv[0:1] = c_send[row_of(s)]
    pltpu.make_async_copy(c_recv.at[1:256], c_recv.at[1:256], c_rsem).wait()
    summed = c_recv[0:64] + c_recv[64:128] + c_recv[128:192] + c_recv[192:256]
    summed = jnp.concatenate([summed, jnp.zeros((64, 128), F32)], axis=0).T
    values = summed[0:16] + pltpu.roll(summed[16:32], 64, 1)
    out_ref[...] = values
    for copy in step_copies + a_copies + b_copies:
        copy.wait_send()
    pltpu.make_async_copy(c_recv.at[1:256], c_recv.at[1:256], c_ssem).wait()


def paint(values_ref, cos_ref, sin_ref, high_ref, low_ref, out_hbm, pieces, sem):
    values = values_ref[...]
    swapped = pltpu.roll(values, 64, 1)
    fine_hi, fine_lo = high_ref[...], low_ref[...]
    copies = []
    for piece in range(4):
        moved = jnp.concatenate(
            [
                values * cos_ref[a : a + 1] + swapped * sin_ref[a : a + 1]
                for a in range(piece * 8, piece * 8 + 8)
            ],
            axis=0,
        )
        moved_hi, moved_lo = split(moved)
        image = jnp.dot(moved_hi, fine_hi, preferred_element_type=F32)
        image = image + jnp.dot(moved_lo, fine_hi, preferred_element_type=F32)
        image = image + jnp.dot(moved_hi, fine_lo, preferred_element_type=F32)
        for a in range(8):
            pieces[piece, :, a * 128 : a * 128 + 128] = image[a * 16 : a * 16 + 16]
        copy = pltpu.make_async_copy(
            pieces.at[piece], out_hbm.at[:, piece * 1024 : piece * 1024 + 1024], sem.at[piece]
        )
        copy.start()
        copies.append(copy)
    for copy in copies:
        copy.wait()


def local(vis, counts, band_start, beam, legendre, cycle_index):
    anywhere = pl.BlockSpec(memory_space=pl.ANY)
    dma = pltpu.SemaphoreType.DMA
    vmem = pl.BlockSpec(memory_space=pltpu.VMEM)
    tables = pl.pallas_call(
        body,
        out_shape=(
            pltpu.VMEM((16, 128), F32),
            pltpu.VMEM((32, 128), F32),
            pltpu.VMEM((32, 128), F32),
            pltpu.VMEM((128, 128), BF16),
            pltpu.VMEM((128, 128), BF16),
        ),
        in_specs=[
            anywhere,
            anywhere,
            anywhere,
            anywhere,
            anywhere,
            anywhere,
        ],
        out_specs=[vmem] * 5,
        scratch_shapes=[
            pltpu.VMEM((2, 32, 1024), F32),
            pltpu.VMEM((8, 128), I32),
            pltpu.SMEM((1,), I32),
            pltpu.VMEM((2, 1024, 1024), BF16),
            pltpu.VMEM((1024, 1024), BF16),
            pltpu.VMEM((8, 128), I32),
            pltpu.VMEM((1024, 1024), BF16),
            pltpu.VMEM((1024, 1024), BF16),
            pltpu.VMEM((2048, 1024), BF16),
            pltpu.VMEM((16, 16, 512), jnp.int16),
            pltpu.VMEM((16, 16, 512), jnp.int16),
            pltpu.VMEM((16, 1, 128), F32),
            pltpu.VMEM((16, 1, 128), F32),
            pltpu.VMEM((4, 2, 1024), F32),
            pltpu.VMEM((4, 2, 1024), F32),
            pltpu.VMEM((64, 1, 128), F32),
            pltpu.VMEM((256, 128), F32),
            dma((7,)),
            dma((16,)),
            dma((16,)),
            dma((16,)),
            dma((16,)),
            dma((4,)),
            dma((4,)),
            dma,
            dma,
        ],
        compiler_params=pltpu.CompilerParams(
            collective_id=0, has_side_effects=True, vmem_limit_bytes=56 * 1024 * 1024
        ),
    )(
        vis,
        counts.reshape(8, 128),
        band_start,
        beam,
        legendre,
        cycle_index.reshape(8, 128),
    )
    tables = [pltpu.with_memory_space_constraint(table, pltpu.VMEM) for table in tables]
    return pl.pallas_call(
        paint,
        out_shape=jax.ShapeDtypeStruct((16, NPHI), F32),
        in_specs=[vmem] * 5,
        out_specs=anywhere,
        scratch_shapes=[pltpu.VMEM((4, 16, 1024), F32), dma((4,))],
    )(*tables)


def solution(mesh):
    return jax.shard_map(
        local,
        mesh=mesh,
        in_specs=(
            P("freq", None, "shard", None),
            P(),
            P(),
            P("freq", "shard", None, None, None),
            P("shard", None, None),
            P(),
        ),
        out_specs=P("shard", None),
        check_vma=False,
    )
```
